32 devices in a mesh: fsdp: 8 (over z, y), context: 2 (over x), tensor: 2 (over core).
Axes of the slice: x: 2, y: 2, z: 4, core: 2. Of those that a mesh axis runs over, the one named last changes fastest.
Arguments:
- tokens: bfloat16 [16, 2048, 1024], P('fsdp', 'context'), may hold values from -6 to 6
- cotangent: bfloat16 [16, 2048, 1024], P('fsdp', 'context'), may hold values from -6 to 6
- mixer_gain: float32 [1024], replicated, may hold values from 0.1 to 1.9
- w_zx: bfloat16 [1024, 2, 1536], P(('fsdp', 'context'), None, 'tensor'), may hold values from -0.1875 to 0.1875
- w_bc: bfloat16 [1024, 256], P(('fsdp', 'context')), may hold values from -0.1875 to 0.1875
- w_dt: bfloat16 [1024, 24], P(('fsdp', 'context'), 'tensor'), may hold values from -0.1875 to 0.1875
- conv_x: float32 [4, 1536], P(None, 'tensor'), may hold values from -3 to 3
- conv_bc: float32 [4, 256], replicated, may hold values from -3 to 3
- dt_bias: float32 [24], P('tensor'), may hold values from -4 to -1.5
- a_log: float32 [24], P('tensor'), may hold values from -4.6 to 2.3
- skip_scale: float32 [24], P('tensor'), may hold values from 0.5 to 1.5
- mamba_gain: float32 [1536], P('tensor'), may hold values from 0.1 to 1.9
- w_mout: bfloat16 [1024, 1536], P(('fsdp', 'context'), 'tensor'), may hold values from -0.15625 to 0.15625
- w_q: bfloat16 [1024, 512], P(('fsdp', 'context'), 'tensor'), may hold values from -0.1875 to 0.1875
- key_value_weight: bfloat16 [1024, 2, 128], P(('fsdp', 'context'), 'tensor'), may hold values from -0.1875 to 0.1875
- w_o: bfloat16 [1024, 512], P(('fsdp', 'context'), 'tensor'), may hold values from -1 to 1
- ffn_gain: float32 [1024], replicated, may hold values from 0.1 to 1.9
- w_gu: bfloat16 [1024, 2, 2048], P(('fsdp', 'context'), None, 'tensor'), may hold values from -0.1875 to 0.1875
- w_down: bfloat16 [1024, 2048], P(('fsdp', 'context'), 'tensor'), may hold values from -0.125 to 0.125
Outputs:
- outputs: bfloat16 [16, 2048, 1024], P('fsdp', 'context')
- grad_tokens: float32 [16, 2048, 1024], P('fsdp', 'context')
- grad_mixer_gain: float32 [1024], replicated
- grad_w_zx: float32 [1024, 2, 1536], P(('fsdp', 'context'), None, 'tensor')
- grad_w_bc: float32 [1024, 256], P(('fsdp', 'context'))
- grad_w_dt: float32 [1024, 24], P(('fsdp', 'context'), 'tensor')
- grad_conv_x: float32 [4, 1536], P(None, 'tensor')
- grad_conv_bc: float32 [4, 256], replicated
- grad_dt_bias: float32 [24], P('tensor')
- grad_a_log: float32 [24], P('tensor')
- grad_skip_scale: float32 [24], P('tensor')
- grad_mamba_gain: float32 [1536], P('tensor')
- grad_w_mout: float32 [1024, 1536], P(('fsdp', 'context'), 'tensor')
- grad_w_q: float32 [1024, 512], P(('fsdp', 'context'), 'tensor')
- grad_w_kv: float32 [1024, 2, 128], P(('fsdp', 'context'), 'tensor')
- grad_w_o: float32 [1024, 512], P(('fsdp', 'context'), 'tensor')
- grad_ffn_gain: float32 [1024], replicated
- grad_w_gu: float32 [1024, 2, 2048], P(('fsdp', 'context'), None, 'tensor')
- grad_w_down: float32 [1024, 2048], P(('fsdp', 'context'), 'tensor')
The draws below stay inside these ranges and needn't reach their ends.
All inputs are finite; a program needn't handle non-finite values.
Results may differ from the reference program's by a relative error of at most 0.017.
Values may be sent and summed in bfloat16 or wider, within the bound.
A program may use at most 320 MiB of HBM per device.

```python
import jax
import jax.numpy as jnp
from jax import lax

MODEL_WIDTH = 1024
HM = 24
PM = 64
NS = 128
CONV = 4
QUERY_HEADS = 8
KEY_VALUE_HEADS = 2
HEAD_WIDTH = 64
FF = 2048
STRETCH = 128
SEQUENCE_LENGTH = 2048
DM = 1536
SEQS = 16


def steps_of(rng, extent, split, low, high):
    def one(axis_at, blocks):
        heights = jax.random.uniform(jax.random.fold_in(jax.random.fold_in(rng, 6), axis_at), (blocks,), jnp.float32, low / len(split), high / len(split))
        return jnp.repeat(jnp.exp(heights), extent[axis_at] // blocks).reshape((-1,) + (1,) * (len(extent) - axis_at - 1))

    gain = one(*split[0])
    for cut in split[1:]:
        gain = gain * one(*cut)
    return gain


def centred(key, shape, spread, most, split=(), dtype=jnp.bfloat16):
    gain = steps_of(key, shape, split, -0.22, 0.18) if split else 1.0
    drawn = jax.random.normal(key, shape, jnp.float32) * spread * gain
    return jnp.minimum(jnp.maximum(drawn, -most), most).astype(dtype)


def setup_inputs(seed: int = 0) -> dict:
    splits = jax.random.split(jax.random.key(seed), 20)
    tokens = centred(splits[0], (SEQS, SEQUENCE_LENGTH, MODEL_WIDTH), 1.0, 6.0, ((0, 8), (1, 2)))
    cotangent = centred(splits[1], (SEQS, SEQUENCE_LENGTH, MODEL_WIDTH), 1.0, 6.0, ((0, 8), (1, 2)))
    mixer_gain = jnp.clip(1.0 + 0.18 * jax.random.normal(splits[2], (MODEL_WIDTH,), jnp.float32), 0.1, 1.9)
    w_zx = centred(splits[3], (MODEL_WIDTH, 2, DM), MODEL_WIDTH ** -0.5, 0.1875, ((0, 16), (2, 2)))
    w_bc = centred(splits[4], (MODEL_WIDTH, 2 * NS), MODEL_WIDTH ** -0.5, 0.1875, ((0, 16),))
    w_dt = centred(splits[5], (MODEL_WIDTH, HM), MODEL_WIDTH ** -0.5, 0.1875, ((0, 16), (1, 2)))
    conv_x = centred(splits[6], (CONV, DM), CONV ** -0.5, 3.0, ((1, 2),), jnp.float32)
    conv_bc = centred(splits[7], (CONV, 2 * NS), CONV ** -0.5, 3.0, (), jnp.float32)
    dt_bias = jnp.clip(-4.0 + 2.5 * jax.random.uniform(splits[8], (HM,), jnp.float32) ** steps_of(splits[8], (HM,), ((0, 2),), -0.2, 0.2), -4.0, -1.5)
    a_log = jnp.clip(-4.6 + 6.8999998569488525 * jax.random.uniform(splits[9], (HM,), jnp.float32) ** steps_of(splits[9], (HM,), ((0, 2),), -0.2, 0.2), -4.6, 2.3)
    skip_scale = jnp.clip(0.5 + 1.0 * jax.random.uniform(splits[10], (HM,), jnp.float32) ** steps_of(splits[10], (HM,), ((0, 2),), -0.2, 0.2), 0.5, 1.5)
    mamba_gain = jnp.clip(1.0 + 0.18 * jax.random.normal(splits[11], (DM,), jnp.float32), 0.1, 1.9)
    w_mout = centred(splits[12], (MODEL_WIDTH, DM), DM ** -0.5, 0.15625, ((0, 16), (1, 2)))
    w_q = centred(splits[13], (MODEL_WIDTH, QUERY_HEADS * HEAD_WIDTH), MODEL_WIDTH ** -0.5, 0.1875, ((0, 16), (1, 2)))
    key_value_weight = centred(splits[14], (MODEL_WIDTH, KEY_VALUE_HEADS, 2 * HEAD_WIDTH), MODEL_WIDTH ** -0.5, 0.1875, ((0, 16), (1, 2)))
    w_o = centred(splits[15], (MODEL_WIDTH, QUERY_HEADS * HEAD_WIDTH), (HEAD_WIDTH // 2) ** -0.5, 1.0, ((0, 16), (1, 2)))
    ffn_gain = jnp.clip(1.0 + 0.18 * jax.random.normal(splits[16], (MODEL_WIDTH,), jnp.float32), 0.1, 1.9)
    w_gu = centred(splits[17], (MODEL_WIDTH, 2, FF), MODEL_WIDTH ** -0.5, 0.1875, ((0, 16), (2, 2)))
    w_down = centred(splits[18], (MODEL_WIDTH, FF), FF ** -0.5, 0.125, ((0, 16), (1, 2)))
    return {"tokens": tokens, "cotangent": cotangent, "mixer_gain": mixer_gain, "w_zx": w_zx, "w_bc": w_bc, "w_dt": w_dt, "conv_x": conv_x, "conv_bc": conv_bc, "dt_bias": dt_bias, "a_log": a_log, "skip_scale": skip_scale, "mamba_gain": mamba_gain, "w_mout": w_mout, "w_q": w_q, "key_value_weight": key_value_weight, "w_o": w_o, "ffn_gain": ffn_gain, "w_gu": w_gu, "w_down": w_down}


EPS = 1e-05
ROPE_BASE = 100000000000.0
HIGH = lax.Precision.HIGHEST

@jax.custom_vjp
def low(v):
    return lax.optimization_barrier(v.astype(jnp.bfloat16)).astype(jnp.float32)

@jax.custom_vjp
def low_back(v):
    return v

def low_keep(v):
    return (low(v), None)

def low_pass(kept, grad):
    return (grad,)

def back_keep(v):
    return (v, None)

def back_low(kept, grad):
    return (low(grad),)
low.defvjp(low_keep, low_pass)
low_back.defvjp(back_keep, back_low)

def rms_scale(hidden, gain_vec):
    inverse = lax.rsqrt(lax.optimization_barrier(jnp.mean(hidden * hidden, -1, keepdims=True)) + EPS)
    return hidden * inverse * gain_vec

def conv_silu(values, tail_rows, kernel):
    extended = jnp.concatenate([tail_rows, values], 1)
    length = values.shape[1]
    summed = kernel[0] * extended[:, 0:length]
    for offset in range(1, kernel.shape[0]):
        summed = summed + kernel[offset] * extended[:, offset:offset + length]
    return jax.nn.silu(summed)

def ssd_stretch(carried, inputs):
    channels, b_in, c_in, decay_log, dt_step = inputs
    cumulative = jnp.cumsum(decay_log, axis=1)
    distance = cumulative[:, :, None, :] - cumulative[:, None, :, :]
    span_len = cumulative.shape[1]
    steps_row = jnp.arange(span_len).astype(jnp.int32)
    causal = (steps_row[:, None] >= steps_row[None, :])[None, :, :, None]
    within = jnp.where(causal, jnp.exp(jnp.where(causal, distance, 0.0)), 0.0)
    intersection = jnp.einsum('gtn,gsn->gts', c_in, b_in, precision=HIGH)
    mixing = intersection[..., None] * within * dt_step[:, None, :, :]
    result = jnp.einsum('gtsh,gshp->gthp', mixing, channels, precision=HIGH)
    result = result + jnp.exp(cumulative)[..., None] * jnp.einsum('gtn,ghpn->gthp', c_in, carried, precision=HIGH)
    weight_end = jnp.exp(cumulative[:, -1:, :] - cumulative) * dt_step
    carried = jnp.exp(cumulative[:, -1, :])[..., None, None] * carried + jnp.einsum('gsh,gshp,gsn->ghpn', weight_end, channels, b_in, precision=HIGH)
    return (carried, result)

def stretch_run(initial, channels, b_in, c_in, decay_log, dt_step):
    local_sequences, length = (channels.shape[0], channels.shape[1])
    blocks = length // STRETCH

    def split_blocks(array):
        return jnp.moveaxis(array.reshape((local_sequences, blocks, STRETCH) + array.shape[2:]), 1, 0)
    final, pieces = lax.scan(jax.checkpoint(ssd_stretch), initial, (split_blocks(channels), split_blocks(b_in), split_blocks(c_in), split_blocks(decay_log), split_blocks(dt_step)))
    return (final, jnp.moveaxis(pieces, 0, 1).reshape(channels.shape))

def rope_tables(length):
    position = jnp.arange(length).astype(jnp.int32).astype(jnp.float32)
    frequency = jnp.exp(-jnp.log(ROPE_BASE) * jnp.arange(0, HEAD_WIDTH, 2).astype(jnp.float32) / HEAD_WIDTH)
    angles = position[:, None] * frequency[None, :]
    return (jnp.cos(angles)[:, None, :], jnp.sin(angles)[:, None, :])

def rotate(values, cosine, sine_val):
    first_half, second_half = (values[..., :HEAD_WIDTH // 2], values[..., HEAD_WIDTH // 2:])
    return jnp.concatenate([first_half * cosine - second_half * sine_val, second_half * cosine + first_half * sine_val], -1)

def mixer_layer(weights, hidden):
    mixer_gain, w_zx, w_bc, w_dt, conv_x, conv_bc, dt_bias, a_log, skip_scale, mamba_gain, w_mout, w_q, key_value_weight, w_o, ffn_gain, w_gu, w_down = weights
    local_sequences = hidden.shape[0]
    normed = low(rms_scale(hidden, mixer_gain))
    zx_proj = low_back(jnp.einsum('gtd,dkc->gtkc', normed, w_zx, precision=HIGH))
    z_proj, x_proj = (zx_proj[:, :, 0], zx_proj[:, :, 1])
    bc_proj = low_back(jnp.einsum('gtd,dc->gtc', normed, w_bc, precision=HIGH))
    dt_proj = low_back(jnp.einsum('gtd,dc->gtc', normed, w_dt, precision=HIGH))
    x_conv = conv_silu(x_proj, jnp.zeros((local_sequences, CONV - 1, DM), jnp.float32), conv_x)
    bc_conv = conv_silu(bc_proj, jnp.zeros((local_sequences, CONV - 1, 2 * NS), jnp.float32), conv_bc)
    b_in, c_in = (bc_conv[..., :NS], bc_conv[..., NS:])
    dt_step = jax.nn.softplus(dt_proj + dt_bias)
    decay_log = -jnp.exp(a_log) * dt_step
    channels = x_conv.reshape(local_sequences, SEQUENCE_LENGTH, HM, PM)
    zero_state = jnp.zeros((local_sequences, HM, PM, NS), jnp.float32)
    final, pieces = stretch_run(zero_state, channels, b_in, c_in, decay_log, dt_step)
    ssm_out = pieces + skip_scale[:, None] * channels
    gated = ssm_out.reshape(local_sequences, SEQUENCE_LENGTH, DM) * jax.nn.silu(z_proj)
    halves = gated.reshape(local_sequences, SEQUENCE_LENGTH, 2, DM // 2)
    halves = halves * lax.rsqrt(lax.optimization_barrier(jnp.mean(halves * halves, -1, keepdims=True)) + EPS)
    mamba_act = low(halves.reshape(local_sequences, SEQUENCE_LENGTH, DM) * mamba_gain)
    mamba_out = jnp.einsum('gtc,dc->gtd', mamba_act, w_mout, precision=HIGH)
    q_proj = low_back(jnp.einsum('gtd,dc->gtc', normed, w_q, precision=HIGH))
    kv_proj = low_back(jnp.einsum('gtd,djc->gtjc', normed, key_value_weight, precision=HIGH))
    cosine, sine_val = rope_tables(SEQUENCE_LENGTH)
    query_rows = low(rotate(q_proj.reshape(local_sequences, SEQUENCE_LENGTH, QUERY_HEADS, HEAD_WIDTH), cosine, sine_val))
    keys_all = low(rotate(kv_proj[..., :HEAD_WIDTH], cosine, sine_val))
    values_all = low(kv_proj[..., HEAD_WIDTH:])
    query_block = min(512, SEQUENCE_LENGTH)
    grouped_heads = query_rows.reshape(local_sequences, SEQUENCE_LENGTH // query_block, query_block, KEY_VALUE_HEADS, QUERY_HEADS // KEY_VALUE_HEADS, HEAD_WIDTH)
    grouped_heads = jnp.moveaxis(grouped_heads, 1, 0)
    key_index = jnp.arange(SEQUENCE_LENGTH).astype(jnp.int32)

    def attend(inputs):
        block_q, block_first = inputs
        scores = low_back(jnp.einsum('gqjed,gkjd->gjeqk', block_q, keys_all, precision=HIGH) * HEAD_WIDTH ** (-0.5))
        query_index = block_first + jnp.arange(query_block).astype(jnp.int32)
        allowed = query_index[:, None] >= key_index[None, :]
        masked = jnp.where(allowed, scores, 0.0)
        row_max = lax.optimization_barrier(jnp.max(jnp.where(allowed, scores, lax.optimization_barrier(jnp.min(scores, -1, keepdims=True))), -1, keepdims=True))
        exp_vals = jnp.where(allowed, jnp.exp(masked - row_max), 0.0)
        probs = exp_vals / lax.optimization_barrier(jnp.sum(exp_vals, -1, keepdims=True))
        return jnp.einsum('gjeqk,gkjd->gqjed', low(probs), values_all, precision=HIGH)
    block_starts = (jnp.arange(SEQUENCE_LENGTH // query_block) * query_block).astype(jnp.int32)
    attended = lax.map(jax.checkpoint(attend), (grouped_heads, block_starts))
    attended = jnp.moveaxis(attended, 0, 1).reshape(local_sequences, SEQUENCE_LENGTH, QUERY_HEADS * HEAD_WIDTH)
    att_act = low(low_back(attended))
    attn_out = jnp.einsum('gtc,dc->gtd', att_act, w_o, precision=HIGH)
    residual = hidden + low_back(mamba_out + attn_out)
    normed_two = low(rms_scale(residual, ffn_gain))
    gu_proj = low_back(jnp.einsum('gtd,dkf->gtkf', normed_two, w_gu, precision=HIGH))
    activation = low(jax.nn.silu(gu_proj[:, :, 0]) * gu_proj[:, :, 1])
    down_sum = low_back(jnp.einsum('gtf,df->gtd', activation, w_down, precision=HIGH))
    return residual + down_sum

def reference(tokens, cotangent, mixer_gain, w_zx, w_bc, w_dt, conv_x, conv_bc, dt_bias, a_log, skip_scale, mamba_gain, w_mout, w_q, key_value_weight, w_o, ffn_gain, w_gu, w_down):
    weights = tuple((array.astype(jnp.float32) for array in (mixer_gain, w_zx, w_bc, w_dt, conv_x, conv_bc, dt_bias, a_log, skip_scale, mamba_gain, w_mout, w_q, key_value_weight, w_o, ffn_gain, w_gu, w_down)))
    pair_count = SEQS // 2
    tokens_pairs = tokens.astype(jnp.float32).reshape(pair_count, 2, SEQUENCE_LENGTH, MODEL_WIDTH)
    cot_pairs = cotangent.astype(jnp.float32).reshape(pair_count, 2, SEQUENCE_LENGTH, MODEL_WIDTH)

    def one_pair(running, inputs):
        block_in, block_cot = inputs
        result, back_fn = jax.vjp(mixer_layer, weights, block_in)
        grad_weights, grad_in = back_fn(block_cot)
        running = jax.tree.map(jnp.add, running, grad_weights)
        return (running, (result.astype(jnp.bfloat16), grad_in))
    zero_grads = jax.tree.map(jnp.zeros_like, weights)
    totals, (results, grad_inputs) = lax.scan(one_pair, zero_grads, (tokens_pairs, cot_pairs))
    return (results.reshape(SEQS, SEQUENCE_LENGTH, MODEL_WIDTH), grad_inputs.reshape(SEQS, SEQUENCE_LENGTH, MODEL_WIDTH), totals[0], totals[1], totals[2], totals[3], totals[4], totals[5], totals[6], totals[7], totals[8], totals[9], totals[10], totals[11], totals[12], totals[13], totals[14], totals[15], totals[16])
```

```python
import functools

import jax
import jax.numpy as jnp
from jax import lax
from jax.experimental import pallas as pl
from jax.experimental.pallas import tpu as pltpu
from jax.sharding import PartitionSpec as P

PM = 64
NS = 128
CONV = 4
HEAD_WIDTH = 64
STRETCH = 128
SEQUENCE_LENGTH = 2048


EPS = 1e-05
ROPE_BASE = 100000000000.0
HIGH = lax.Precision.HIGHEST
BIG = -1e30


def passed_along(block, axis, distance):
    devices = range(lax.axis_size(axis))
    route = [(i - distance, i) for i in devices if i - distance in devices]
    return lax.ppermute(block, axis, route)


def rms_scale(hidden, gain_vec):
    inverse = lax.rsqrt(jnp.mean(hidden * hidden, -1, keepdims=True) + EPS)
    return hidden * inverse * gain_vec


def conv_silu(values, tail_rows, kernel):
    extended = jnp.concatenate([tail_rows, values], 1)
    length = values.shape[1]
    summed = kernel[0] * extended[:, 0:length]
    for offset in range(1, kernel.shape[0]):
        summed = summed + kernel[offset] * extended[:, offset : offset + length]
    return jax.nn.silu(summed)


LOW = jnp.bfloat16
VMEM_BYTES = 50 * 1024 * 1024
QUERY_BLOCK = 256


def dot(left, right, left_dim, right_dim):
    return lax.dot_general(
        left, right, (((left_dim,), (right_dim,)), ((), ())), preferred_element_type=jnp.float32
    )


def iotas(rows, cols):
    return (
        lax.broadcasted_iota(jnp.int32, (rows, cols), 0),
        lax.broadcasted_iota(jnp.int32, (rows, cols), 1),
    )


def two_heads(ref, pair, left):
    return jnp.where(
        left, ref[0, :, 2 * pair : 2 * pair + 1], ref[0, :, 2 * pair + 1 : 2 * pair + 2]
    )


def ssd_forward(heads, x_ref, b_ref, c_ref, cum_ref, dt_ref, cumt_ref, dtt_ref, init_ref, y_ref, saved_ref, state):
    @pl.when(pl.program_id(1) == 0)
    def first():
        state[...] = init_ref[0]

    saved_ref[0] = state[...]
    b_low = b_ref[0].astype(LOW)
    c_low = c_ref[0].astype(LOW)
    meet = dot(c_low, b_low, 1, 1)
    rows, cols = iotas(STRETCH, 2 * PM)
    causal = rows >= cols
    left = cols < PM
    for pair in range(heads // 2):
        span = slice(2 * PM * pair, 2 * PM * (pair + 1))
        x = x_ref[0, :, span]
        x_low = x.astype(LOW)
        held = state[:, span]
        parts = []
        for head in (2 * pair, 2 * pair + 1):
            gap = cum_ref[0, :, head : head + 1] - cumt_ref[0, head : head + 1, :]
            within = jnp.exp(jnp.where(causal, gap, BIG))
            mixing = meet * within * dtt_ref[0, head : head + 1, :]
            parts.append(dot(mixing.astype(LOW), x_low, 1, 0))
        cum = two_heads(cum_ref, pair, left)
        end = cum[STRETCH - 1 : STRETCH, :]
        y_ref[0, :, span] = jnp.where(left, parts[0], parts[1]) + jnp.exp(cum) * dot(
            c_low, held.astype(LOW), 1, 0
        )
        weighted = jnp.exp(end - cum) * two_heads(dt_ref, pair, left) * x
        state[:, span] = jnp.exp(end) * held + dot(b_low, weighted.astype(LOW), 0, 0)


def ssd_backward(heads, x_ref, dy_ref, b_ref, c_ref, cum_ref, dt_ref, cumt_ref, dtt_ref, saved_ref, last_ref, dx_ref, db_ref, dc_ref, dcum_ref, ddt_ref, ddtt_ref, state):
    @pl.when(pl.program_id(1) == 0)
    def first():
        state[...] = last_ref[0]

    b_low = b_ref[0].astype(LOW)
    c_low = c_ref[0].astype(LOW)
    meet = dot(c_low, b_low, 1, 1)
    rows, cols = iotas(STRETCH, 2 * PM)
    causal = rows >= cols
    left = cols < PM
    last_row = lax.broadcasted_iota(jnp.int32, (STRETCH, 1), 0) == STRETCH - 1
    grad_meet = jnp.zeros((STRETCH, STRETCH), jnp.float32)
    grad_b = jnp.zeros((STRETCH, NS), jnp.float32)
    grad_c = jnp.zeros((STRETCH, NS), jnp.float32)
    for pair in range(heads // 2):
        span = slice(2 * PM * pair, 2 * PM * (pair + 1))
        x = x_ref[0, :, span]
        dy = dy_ref[0, :, span]
        x_low = x.astype(LOW)
        dy_low = dy.astype(LOW)
        held = saved_ref[0, :, span]
        held_low = held.astype(LOW)
        grad_state = state[:, span]
        grad_low = grad_state.astype(LOW)
        cum = two_heads(cum_ref, pair, left)
        end = cum[STRETCH - 1 : STRETCH, :]
        from_start = jnp.exp(cum) * dy
        from_start_low = from_start.astype(LOW)
        to_end = jnp.exp(end - cum)
        weight = to_end * two_heads(dt_ref, pair, left)
        crossed = from_start * dot(c_low, held_low, 1, 0)
        back = dot(b_low, grad_low, 1, 0)
        ending = to_end * x * back
        whole = jnp.exp(end) * grad_state * held
        grad_c = grad_c + dot(from_start_low, held_low, 1, 1)
        grad_b = grad_b + dot((weight * x).astype(LOW), grad_low, 1, 1)
        parts = []
        for which in (0, 1):
            head = 2 * pair + which
            mine = left if which == 0 else jnp.logical_not(left)
            dt_row = dtt_ref[0, head : head + 1, :]
            gap = cum_ref[0, :, head : head + 1] - cumt_ref[0, head : head + 1, :]
            within = jnp.exp(jnp.where(causal, gap, BIG))
            scaled = within * dt_row
            grad_mixing = dot(jnp.where(mine, dy, 0.0).astype(LOW), x_low, 1, 1)
            grad_meet = grad_meet + grad_mixing * scaled
            product = grad_mixing * meet * within
            ddtt_ref[0, head : head + 1, :] = jnp.sum(product, 0, keepdims=True)
            parts.append(dot((meet * scaled).astype(LOW), dy_low, 0, 0))
            ends = jnp.sum(jnp.where(mine, ending, 0.0), 1, keepdims=True)
            ddt_ref[0, :, head : head + 1] = ends
            ended = ends * dt_ref[0, :, head : head + 1]
            total = jnp.sum(ended, 0, keepdims=True) + jnp.sum(
                jnp.sum(jnp.where(mine, whole, 0.0), 1, keepdims=True), 0, keepdims=True
            )
            dcum_ref[0, :, head : head + 1] = (
                jnp.sum(product * dt_row + jnp.where(mine, crossed, 0.0), 1, keepdims=True)
                - ended
                + jnp.where(last_row, total, 0.0)
            )
        dx_ref[0, :, span] = jnp.where(left, parts[0], parts[1]) + weight * back
        state[:, span] = jnp.exp(end) * grad_state + dot(c_low, from_start_low, 0, 0)
    grad_meet_low = grad_meet.astype(LOW)
    db_ref[0] = grad_b + dot(grad_meet_low, c_low, 0, 0)
    dc_ref[0] = grad_c + dot(grad_meet_low, b_low, 1, 0)


def ssd_call(backward, operands):
    x = operands[0]
    seqs, length, width = x.shape
    heads = width // PM
    blocks = length // STRETCH
    at = (lambda c: blocks - 1 - c) if backward else (lambda c: c)
    wide = pl.BlockSpec((1, STRETCH, width), lambda s, c: (s, at(c), 0))
    b_spec = pl.BlockSpec((1, STRETCH, NS), lambda s, c: (s, at(c), 0))
    c_spec = pl.BlockSpec((1, STRETCH, NS), lambda s, c: (s, at(c), 1))
    per_head = pl.BlockSpec((1, STRETCH, heads), lambda s, c: (s, at(c), 0))
    turned = pl.BlockSpec((1, heads, STRETCH), lambda s, c: (s, 0, at(c)))
    kept = pl.BlockSpec((1, NS, width), lambda s, c: (s, at(c), 0))
    once = pl.BlockSpec((1, NS, width), lambda s, c: (s, 0, 0))

    def shape(*dims):
        return jax.ShapeDtypeStruct((seqs,) + dims, jnp.float32)

    if backward:
        in_specs = [wide, wide, b_spec, c_spec, per_head, per_head, turned, turned, kept, once]
        out_specs = [wide, b_spec, b_spec, per_head, per_head, turned]
        out_shape = [
            shape(length, width),
            shape(length, NS),
            shape(length, NS),
            shape(length, heads),
            shape(length, heads),
            shape(heads, length),
        ]
    else:
        in_specs = [wide, b_spec, c_spec, per_head, per_head, turned, turned, once]
        out_specs = [wide, kept]
        out_shape = [shape(length, width), shape(blocks * NS, width)]
    return pl.pallas_call(
        functools.partial(ssd_backward if backward else ssd_forward, heads),
        grid=(seqs, blocks),
        in_specs=in_specs,
        out_specs=out_specs,
        out_shape=out_shape,
        scratch_shapes=[pltpu.VMEM((NS, width), jnp.float32)],
        compiler_params=pltpu.CompilerParams(vmem_limit_bytes=VMEM_BYTES),
    )(*operands)


def attention_forward(scale, first_ref, q_ref, k_ref, v_ref, out_ref):
    scores = dot(q_ref[0, 0], k_ref[0], 1, 1) * scale
    rows, cols = iotas(*scores.shape)
    begin = first_ref[0] + pl.program_id(2) * q_ref.shape[2]
    scores = jnp.where(rows + begin >= cols, scores, BIG)
    raised = jnp.exp(scores - jnp.max(scores, 1, keepdims=True))
    total = jnp.sum(raised, 1, keepdims=True)
    out_ref[0, 0] = dot(raised.astype(LOW), v_ref[0], 1, 0) / total


def attention_backward(scale, first_ref, q_ref, k_ref, v_ref, grad_ref, dq_ref, dk_ref, dv_ref):
    @pl.when((pl.program_id(1) == 0) & (pl.program_id(2) == 0))
    def first():
        dk_ref[...] = jnp.zeros_like(dk_ref)
        dv_ref[...] = jnp.zeros_like(dv_ref)

    q, k, grad = (q_ref[0, 0], k_ref[0], grad_ref[0, 0])
    scores = dot(k, q, 1, 1) * scale
    rows, cols = iotas(*scores.shape)
    begin = first_ref[0] + pl.program_id(2) * q_ref.shape[2]
    scores = jnp.where(cols + begin >= rows, scores, BIG)
    raised = jnp.exp(scores - jnp.max(scores, 0, keepdims=True))
    probs = raised * (1.0 / jnp.sum(raised, 0, keepdims=True))
    grad_probs = dot(v_ref[0], grad, 1, 1)
    mean = jnp.sum(probs * grad_probs, 0, keepdims=True)
    grad_scores = (probs * (grad_probs - mean)).astype(LOW)
    dq_ref[0, 0] = dot(grad_scores, k, 0, 0) * scale
    dk_ref[0] += dot(grad_scores, q, 1, 0) * scale
    dv_ref[0] += dot(probs.astype(LOW), grad, 1, 0)


def attention_call(first_pos, q, k, v, grad=None):
    groups, heads, length, width = q.shape
    keys = k.shape[1]
    block = min(QUERY_BLOCK, length)
    rows = pl.BlockSpec((1, 1, block, width), lambda g, e, i: (g, e, i, 0))
    whole = pl.BlockSpec((1, keys, width), lambda g, e, i: (g, 0, 0))
    place = pl.BlockSpec(memory_space=pltpu.SMEM)
    like_q = jax.ShapeDtypeStruct(q.shape, jnp.float32)
    like_k = jax.ShapeDtypeStruct(k.shape, jnp.float32)
    backward = grad is not None
    return pl.pallas_call(
        functools.partial(
            attention_backward if backward else attention_forward, HEAD_WIDTH ** (-0.5)
        ),
        grid=(groups, heads, length // block),
        in_specs=[place, rows, whole, whole] + ([rows] if backward else []),
        out_specs=[rows, whole, whole] if backward else rows,
        out_shape=[like_q, like_k, like_k] if backward else like_q,
        compiler_params=pltpu.CompilerParams(vmem_limit_bytes=VMEM_BYTES),
    )(jnp.reshape(first_pos, (1,)).astype(jnp.int32), q, k, v, *([grad] if backward else []))


def gated_norm(ssm_out, z_proj, gain_vec):
    return rms_scale(ssm_out * jax.nn.silu(z_proj), gain_vec)


def chained(through, state, axis, reverse):
    count = lax.axis_size(axis)
    place = lax.axis_index(axis)
    all_through = lax.all_gather(through, axis)
    all_state = lax.all_gather(state.astype(LOW), axis)
    result = jnp.zeros_like(state)
    for step in range(count - 1):
        source = count - 1 - step if reverse else step
        joined = all_through[source][:, None, :] * result + all_state[source].astype(jnp.float32)
        counts = source > place if reverse else source < place
        result = jnp.where(counts, joined, result)
    return result


def rope_tables(first_pos, length):
    position = (first_pos + jnp.arange(length)).astype(jnp.float32)
    frequency = jnp.exp(
        -jnp.log(ROPE_BASE) * jnp.arange(0, HEAD_WIDTH, 2).astype(jnp.float32) / HEAD_WIDTH
    )
    angles = position[:, None] * frequency[None, :]
    return (jnp.cos(angles)[:, None, :], jnp.sin(angles)[:, None, :])


def rotate(values, cosine, sine_val):
    first_half, second_half = (values[..., : HEAD_WIDTH // 2], values[..., HEAD_WIDTH // 2 :])
    return jnp.concatenate(
        [
            first_half * cosine - second_half * sine_val,
            second_half * cosine + first_half * sine_val,
        ],
        -1,
    )


def unrotate(values, cosine, sine_val):
    first_half, second_half = (values[..., : HEAD_WIDTH // 2], values[..., HEAD_WIDTH // 2 :])
    return jnp.concatenate(
        [
            first_half * cosine + second_half * sine_val,
            second_half * cosine - first_half * sine_val,
        ],
        -1,
    )


def body(
    tokens,
    cotangent,
    mixer_gain,
    w_zx,
    w_bc,
    w_dt,
    conv_x,
    conv_bc,
    dt_bias,
    a_log,
    skip_scale,
    mamba_gain,
    w_mout,
    w_q,
    key_value_weight,
    w_o,
    ffn_gain,
    w_gu,
    w_down,
):
    seqs, length, model = tokens.shape
    hidden = tokens.astype(jnp.float32)
    shard = w_zx.shape[0]
    inner = w_zx.shape[2]
    heads = dt_bias.shape[0]
    kv_heads = key_value_weight.shape[1]
    q_width = w_q.shape[1]
    q_heads = q_width // HEAD_WIDTH
    group_size = q_heads // kv_heads
    kv_width = kv_heads * 2 * HEAD_WIDTH
    ff = w_down.shape[1]
    rows_axes = ("fsdp", "context")

    full_in = lax.all_gather(
        jnp.concatenate(
            [
                w_zx.reshape(shard, 2 * inner),
                w_bc,
                w_q,
                key_value_weight.reshape(shard, kv_width),
                w_dt,
            ],
            1,
        ),
        rows_axes,
        axis=0,
        tiled=True,
    )
    full_out = lax.all_gather(
        jnp.concatenate([w_mout, w_o, w_gu.reshape(shard, 2 * ff), w_down], 1),
        rows_axes,
        axis=0,
        tiled=True,
    )
    cuts_in = [2 * inner, 2 * NS, q_width, kv_width, heads]
    ends_in = [sum(cuts_in[: i + 1]) for i in range(len(cuts_in))]
    full_mout = full_out[:, :inner]
    full_o = full_out[:, inner : inner + q_width]
    full_gu = full_out[:, inner + q_width : inner + q_width + 2 * ff]
    full_down = full_out[:, inner + q_width + 2 * ff :]

    def mult(a, b, dims):
        return jnp.einsum(dims, a, b, preferred_element_type=jnp.float32)

    normed = rms_scale(hidden, mixer_gain).astype(LOW)
    proj = mult(normed, full_in, "std,dc->stc")
    z_proj = proj[..., :inner]
    x_proj = proj[..., inner : 2 * inner]
    bc_proj = proj[..., ends_in[0] : ends_in[1]]
    q_proj = proj[..., ends_in[1] : ends_in[2]]
    kv_proj = proj[..., ends_in[2] : ends_in[3]].reshape(seqs, length, kv_heads, 2 * HEAD_WIDTH)
    dt_proj = proj[..., ends_in[3] :]

    first_pos = lax.axis_index("context") * length
    cosine, sine_val = rope_tables(first_pos, length)
    queries = rotate(q_proj.reshape(seqs, length, q_heads, HEAD_WIDTH), cosine, sine_val).astype(
        LOW
    )
    keys_here = rotate(kv_proj[..., :HEAD_WIDTH], cosine, sine_val).astype(LOW)
    kv_here = jnp.concatenate([keys_here, kv_proj[..., HEAD_WIDTH:].astype(LOW)], -1)
    kv_all = lax.all_gather(jnp.moveaxis(kv_here, 2, 1), "context", axis=2, tiled=True)
    total_len = kv_all.shape[2]
    kv_flat = kv_all.reshape(seqs * kv_heads, total_len, 2 * HEAD_WIDTH)
    k_flat, v_flat = (kv_flat[..., :HEAD_WIDTH], kv_flat[..., HEAD_WIDTH:])

    def to_groups(rows):
        split = rows.reshape(seqs, length, kv_heads, group_size, HEAD_WIDTH)
        return jnp.moveaxis(split, 1, 3).reshape(
            seqs * kv_heads, group_size, length, HEAD_WIDTH
        )

    def from_groups(array):
        split = array.reshape(seqs, kv_heads, group_size, length, HEAD_WIDTH)
        return jnp.moveaxis(split, 3, 1).reshape(seqs, length, q_heads, HEAD_WIDTH)

    q_groups = to_groups(queries)

    tail_x, tail_bc = passed_along(
        (x_proj[:, length - CONV + 1 :], bc_proj[:, length - CONV + 1 :]), "context", 1
    )
    bc_conv = conv_silu(bc_proj, tail_bc, conv_bc)
    x_conv = conv_silu(x_proj, tail_x, conv_x)
    dt_step = jax.nn.softplus(dt_proj + dt_bias)
    rate = -jnp.exp(a_log)
    decay_log = rate * dt_step
    blocks = length // STRETCH
    lower = jnp.tril(jnp.ones((STRETCH, STRETCH), jnp.float32))
    cum_blocks = jnp.einsum(
        "tu,scuh->scth", lower, decay_log.reshape(seqs, blocks, STRETCH, heads), precision=HIGH
    )
    block_ends = cum_blocks[:, :, -1]
    before = jnp.stack(
        [jnp.sum(block_ends[:, :i], 1) if i else jnp.zeros_like(block_ends[:, 0]) for i in range(blocks)],
        1,
    )
    cum_all = (cum_blocks + before[:, :, None]).reshape(seqs, length, heads)
    cum = cum_blocks.reshape(seqs, length, heads)
    cum_turned = jnp.swapaxes(cum, 1, 2)
    dt_turned = jnp.swapaxes(dt_step, 1, 2)
    total = jnp.sum(block_ends, 1)
    spread = jnp.repeat(jnp.eye(heads, dtype=jnp.float32), PM, axis=1)

    def wide(per_head):
        return jnp.einsum("sth,hk->stk", per_head, spread, precision=HIGH)

    b_low = bc_conv[..., :NS].astype(LOW)
    c_low = bc_conv[..., NS:].astype(LOW)
    ending = (wide(jnp.exp(total[:, None] - cum_all) * dt_step) * x_conv).astype(LOW)
    local_end = mult(b_low, ending, "stn,stk->snk")
    through = wide(jnp.exp(total)[:, None])[:, 0]
    incoming = chained(through, local_end, "context", False)
    scan_in = (bc_conv, bc_conv, cum, dt_step, cum_turned, dt_turned)
    pieces, saved = ssd_call(False, (x_conv,) + scan_in + (incoming,))
    skip_wide = jnp.repeat(skip_scale, PM)
    ssm_out = pieces + skip_wide * x_conv
    mamba_f32, gated_back = jax.vjp(gated_norm, ssm_out, z_proj, mamba_gain)
    mamba_act = mamba_f32.astype(LOW)

    attended = attention_call(first_pos, q_groups, k_flat, v_flat)
    att_act = from_groups(attended.astype(LOW)).reshape(seqs, length, q_width)
    mixed = mult(mamba_act, full_mout, "stc,dc->std") + mult(att_act, full_o, "stc,dc->std")
    residual = hidden + lax.psum(mixed.astype(LOW), "tensor").astype(jnp.float32)

    normed_two = rms_scale(residual, ffn_gain).astype(LOW)
    gu_proj = mult(normed_two, full_gu, "std,df->stf")
    gate_val, up_val = (gu_proj[..., :ff], gu_proj[..., ff:])
    gate_sig = jax.nn.sigmoid(gate_val)
    activation = (gate_val * gate_sig * up_val).astype(LOW)
    down_part = mult(activation, full_down, "stf,df->std")
    outputs = (residual + lax.psum(down_part.astype(LOW), "tensor").astype(jnp.float32)).astype(LOW)
    grad_act = mult(cotangent, full_down, "std,df->stf")
    grad_gate = grad_act * up_val * gate_sig * (1.0 + gate_val * (1.0 - gate_sig))
    grad_up = grad_act * gate_val * gate_sig
    grad_gu_act = jnp.concatenate([grad_gate.astype(LOW), grad_up.astype(LOW)], -1)
    part_two = mult(grad_gu_act, full_gu, "stf,df->std")
    d_normed_two = lax.psum(part_two.astype(LOW), "tensor").astype(jnp.float32)

    def scattered(grads):
        return lax.psum_scatter(
            jnp.concatenate([g.astype(LOW) for g in grads], 1),
            rows_axes,
            scatter_dimension=0,
            tiled=True,
        ).astype(jnp.float32)

    shard_ffn = scattered(
        [
            mult(normed_two, grad_gu_act, "std,stf->df"),
            mult(cotangent, activation, "std,stf->df"),
        ]
    )
    residual_back, ffn_back = jax.vjp(rms_scale, residual, ffn_gain)[1](d_normed_two)
    grad_residual = cotangent.astype(jnp.float32) + residual_back
    grad_mix = grad_residual.astype(LOW)
    shard_mix = scattered(
        [mult(grad_mix, mamba_act, "std,stc->dc"), mult(grad_mix, att_act, "std,stc->dc")]
    )

    grad_att = to_groups(mult(grad_mix, full_o, "std,dc->stc").astype(LOW))
    dq, dk, dv = attention_call(first_pos, q_groups, k_flat, v_flat, grad_att)
    kv_grads = jnp.concatenate([dk, dv], -1).reshape(seqs, kv_heads, total_len, 2 * HEAD_WIDTH)
    grad_kv_here = jnp.moveaxis(
        lax.psum_scatter(
            kv_grads.astype(LOW), "context", scatter_dimension=2, tiled=True
        ).astype(jnp.float32),
        1,
        2,
    )
    grad_q_low = (
        unrotate(from_groups(dq), cosine, sine_val).reshape(seqs, length, q_width).astype(LOW)
    )
    grad_kv_low = (
        jnp.concatenate(
            [
                unrotate(grad_kv_here[..., :HEAD_WIDTH], cosine, sine_val),
                grad_kv_here[..., HEAD_WIDTH:],
            ],
            -1,
        )
        .astype(LOW)
        .reshape(seqs, length, kv_width)
    )

    grad_ssm, g_z, g_gain = gated_back(mult(grad_mix, full_mout, "std,dc->stc"))
    starting = (wide(jnp.exp(cum_all)) * grad_ssm).astype(LOW)
    local_start = mult(c_low, starting, "stn,stk->snk")
    later_grad = chained(through, local_start, "context", True)
    dx, db, dc, dcum, ddt, ddt_turned = ssd_call(
        True, (x_conv, grad_ssm) + scan_in + (saved, later_grad)
    )
    ddt_within = jnp.swapaxes(ddt_turned, 1, 2)
    dcum = dcum - dt_step * ddt_within
    g_decay = jnp.einsum(
        "tu,scth->scuh", lower, dcum.reshape(seqs, blocks, STRETCH, heads), precision=HIGH
    ).reshape(seqs, length, heads)
    g_step = ddt + ddt_within + rate * g_decay
    g_dt = g_step * jax.nn.sigmoid(dt_proj + dt_bias)
    g_dt_bias = jnp.sum(g_dt, (0, 1))
    g_a_log = jnp.sum(g_decay * decay_log, (0, 1))
    g_skip = jnp.sum(jnp.sum(grad_ssm * x_conv, (0, 1)).reshape(heads, PM), 1)
    g_x, g_tail_x, g_conv_x = jax.vjp(conv_silu, x_proj, tail_x, conv_x)[1](
        dx + skip_wide * grad_ssm
    )
    g_bc, g_tail_bc, g_conv_bc = jax.vjp(conv_silu, bc_proj, tail_bc, conv_bc)[1](
        jnp.concatenate([db, dc], -1)
    )
    from_next_x, from_next_bc = passed_along((g_tail_x, g_tail_bc), "context", -1)
    pad_rows = ((0, 0), (length - CONV + 1, 0), (0, 0))
    grad_proj = jnp.concatenate(
        [
            g_z.astype(LOW),
            (g_x + jnp.pad(from_next_x, pad_rows)).astype(LOW),
            (g_bc + jnp.pad(from_next_bc, pad_rows)).astype(LOW),
            grad_q_low,
            grad_kv_low,
            g_dt.astype(LOW),
        ],
        -1,
    )
    shard_in = scattered([mult(normed, grad_proj, "std,stc->dc")])
    d_normed = lax.psum(
        mult(grad_proj, full_in, "stc,dc->std").astype(LOW), "tensor"
    ).astype(jnp.float32)
    tokens_back, mixer_back = jax.vjp(rms_scale, hidden, mixer_gain)[1](d_normed)
    grad_tokens = grad_residual + tokens_back

    small = (mixer_back, ffn_back, g_conv_x, g_conv_bc, g_dt_bias, g_a_log, g_skip, g_gain)
    flat = lax.psum(jnp.concatenate([jnp.ravel(a) for a in small]), rows_axes)
    sums = []
    begin = 0
    for a in small:
        sums.append(flat[begin : begin + a.size].reshape(a.shape))
        begin += a.size
    both = lax.psum(
        jnp.concatenate([shard_in[:, ends_in[0] : ends_in[1]], sums[3]], 0), "tensor"
    )
    return (
        outputs,
        grad_tokens,
        sums[0],
        shard_in[:, : ends_in[0]].reshape(shard, 2, inner),
        both[:shard],
        shard_in[:, ends_in[3] :],
        sums[2],
        both[shard:],
        sums[4],
        sums[5],
        sums[6],
        sums[7],
        shard_mix[:, :inner],
        shard_in[:, ends_in[1] : ends_in[2]],
        shard_in[:, ends_in[2] : ends_in[3]].reshape(shard, kv_heads, 2 * HEAD_WIDTH),
        shard_mix[:, inner:],
        sums[1],
        shard_ffn[:, : 2 * ff].reshape(shard, 2, ff),
        shard_ffn[:, 2 * ff :],
    )


def solution(mesh):
    return jax.shard_map(
        body,
        mesh=mesh,
        in_specs=(
            P("fsdp", "context", None),
            P("fsdp", "context", None),
            P(),
            P(("fsdp", "context"), None, "tensor"),
            P(("fsdp", "context"), None),
            P(("fsdp", "context"), "tensor"),
            P(None, "tensor"),
            P(),
            P("tensor"),
            P("tensor"),
            P("tensor"),
            P("tensor"),
            P(("fsdp", "context"), "tensor"),
            P(("fsdp", "context"), "tensor"),
            P(("fsdp", "context"), "tensor", None),
            P(("fsdp", "context"), "tensor"),
            P(),
            P(("fsdp", "context"), None, "tensor"),
            P(("fsdp", "context"), "tensor"),
        ),
        out_specs=(
            P("fsdp", "context", None),
            P("fsdp", "context", None),
            P(),
            P(("fsdp", "context"), None, "tensor"),
            P(("fsdp", "context"), None),
            P(("fsdp", "context"), "tensor"),
            P(None, "tensor"),
            P(),
            P("tensor"),
            P("tensor"),
            P("tensor"),
            P("tensor"),
            P(("fsdp", "context"), "tensor"),
            P(("fsdp", "context"), "tensor"),
            P(("fsdp", "context"), "tensor", None),
            P(("fsdp", "context"), "tensor"),
            P(),
            P(("fsdp", "context"), None, "tensor"),
            P(("fsdp", "context"), "tensor"),
        ),
        check_vma=False,
    )
```
